32 devices in a mesh: layer: 1, energy: 16 (over z, y, core), kpt: 2 (over x).
Axes of the slice: x: 2, y: 2, z: 4, core: 2. Of those that a mesh axis runs over, the one named last changes fastest.
Arguments:
- source: bfloat16 [1, 2, 8, 128, 4, 1024], P('layer', None, 'kpt', 'energy'), may hold values from -6 to 6
- basis: bfloat16 [1, 1024, 1024], P('layer'), may hold values from -0.1875 to 0.1875
- coupling: bfloat16 [1, 1024, 1024], P('layer'), may hold values from -0.25 to 0.25
- levels: float32 [1, 1024], P('layer'), may hold values from -2 to 2
- sigma_real: float32 [1, 128, 1024], P('layer', 'energy'), may hold values from -2.5 to 2.5
- broadening: float32 [1, 128, 1024], P('layer', 'energy'), may hold values from 0.05 to 1
- transverse: float32 [8], P('kpt'), may hold values from -1 to 1
- counts: int32 [1], P('layer'), may hold values from 512 to 1024
- occupation: float32 [128, 4], P('energy'), may hold values from 0.02 to 0.98
- kweight: int32 [8], replicated, may hold values from 1 to 4
- shifts: int32 [512], replicated, may hold values from 1 to 63
- emission: float32 [512], replicated, may hold values from 0.0009765625 to 0.0078125
- absorption: float32 [512], replicated, may hold values from 0.000390625 to 0.00390625
Outputs:
- sigma_lesser: float32 [1, 1024, 128], P('layer', 'energy')
- sigma_greater: float32 [1, 1024, 128], P('layer', 'energy')
The draws below stay inside these ranges and needn't reach their ends.
All inputs are finite; a program needn't handle non-finite values.
Results may differ from the reference program's by a relative error of at most 0.0015.
Values may be sent and summed in bfloat16 or wider, within the bound.
No kernel may reach another device: no remote copies, remote signals or barrier semaphores. Data moves between devices by JAX's collectives and lax.ppermute only.
A program may use at most 64 MiB of HBM per device.

```python
import math
import jax
import jax.numpy as jnp
from jax import lax

NORB = 1024
NPHOT = 512
MODES = 4
LAYERS = 1
ENERGIES = 128
KPTS = 8


def plant(entries, stream_key, least, top_value):
    spot = [jax.random.randint(jax.random.fold_in(stream_key, axis), (), 0, length) for axis, length in enumerate(entries.shape)]
    longest = entries.shape.index(max(entries.shape))
    next_to = spot[:longest] + [(spot[longest] + 1) % entries.shape[longest]] + spot[longest + 1:]
    return entries.at[tuple(spot)].set(least).at[tuple(next_to)].set(top_value)


def steps_of(key, extent, cuts, least, top_value):
    level, own = 1.0, jax.random.fold_in(key, 6)
    for dim, parts in cuts:
        heights = jnp.exp(jax.random.uniform(jax.random.fold_in(own, dim), (parts,), jnp.float32, least / len(cuts), top_value / len(cuts)))
        level = level * jnp.repeat(heights, extent[dim] // parts).reshape([-1 if axis == dim else 1 for axis in range(len(extent))])
    return level


def centred(rng, shape, scale, most, pieces=(), kind=jnp.bfloat16):
    gain = steps_of(rng, shape, pieces, -0.22, 0.18) if pieces else 1.0
    array = jax.random.normal(rng, shape, jnp.float32) * scale * gain
    return jnp.minimum(jnp.maximum(array, -most), most).astype(kind)


def setup_inputs(seed: int = 0) -> dict:
    key_list = jax.random.split(jax.random.key(seed), 14)
    source = centred(key_list[0], (LAYERS, 2, KPTS, ENERGIES, MODES, NORB), 1.0, 6.0, ((2, 2), (3, 16)))
    basis = centred(key_list[1], (LAYERS, NORB, NORB), NORB ** -0.5, 0.1875)
    coupling = centred(key_list[2], (LAYERS, NORB, NORB), (NORB * 4 // 9) ** -0.5, 0.25)
    levels = jnp.clip(jax.random.uniform(key_list[3], (LAYERS, NORB), jnp.float32, -2.0, 2.0), -2.0, 2.0)
    sigma_real = centred(key_list[4], (LAYERS, ENERGIES, NORB), 0.3, 2.5, ((1, 16),), jnp.float32)
    broadening = jnp.clip(jnp.exp(math.log(1.0) - 2.9957323 * jax.random.uniform(key_list[5], (LAYERS, ENERGIES, NORB), jnp.float32) ** steps_of(key_list[5], (LAYERS, ENERGIES, NORB), ((1, 16),), -0.2, 0.2)), 0.05, 1.0)
    transverse = jnp.clip(jax.random.uniform(key_list[6], (KPTS,), jnp.float32, -1.0, 1.0) * steps_of(key_list[6], (KPTS,), ((0, 2),), -0.4, 0.0), -1.0, 1.0)
    counts = jax.random.randint(key_list[7], (LAYERS,), NORB // 2, NORB + 1).astype(jnp.int32)
    occupation = jnp.clip(0.02 + 0.96000002 * jax.random.uniform(key_list[8], (ENERGIES, MODES), jnp.float32) ** steps_of(key_list[8], (ENERGIES, MODES), ((0, 16),), -0.2, 0.2), 0.02, 0.98)
    kweight = plant(jax.random.randint(key_list[9], (KPTS,), 1, 5), jax.random.fold_in(key_list[9], 1), 1, 4).astype(jnp.int32)
    shifts = plant(jax.random.randint(key_list[10], (NPHOT,), 1, ENERGIES // 2), jax.random.fold_in(key_list[10], 1), 1, (ENERGIES // 2) - 1).astype(jnp.int32)
    emission = jnp.clip(jnp.exp(jax.random.uniform(key_list[11], (NPHOT,), jnp.float32, math.log(0.0009765625), math.log(0.0078125))), 0.0009765625, 0.0078125)
    absorption = jnp.clip(jnp.exp(jax.random.uniform(key_list[12], (NPHOT,), jnp.float32, math.log(0.000390625), math.log(0.00390625))), 0.000390625, 0.00390625)
    return dict(source=source, basis=basis, coupling=coupling, levels=levels, sigma_real=sigma_real, broadening=broadening, transverse=transverse, counts=counts, occupation=occupation, kweight=kweight, shifts=shifts, emission=emission, absorption=absorption)


ETA = 1.0


def energy_grid(count):
    return (jnp.arange(count, dtype=jnp.float32) + 0.5) * (4.0 / count) - 2.0


def toeplitz(ahead, behind, count):
    grid = jnp.arange(count, dtype=jnp.int32)
    offset = (grid[None, :] - grid[:, None]).astype(jnp.int32)
    forward = jnp.take(ahead, jnp.clip(offset, 0, count - 1).astype(jnp.int32))
    backward = jnp.take(behind, jnp.clip(-offset, 0, count - 1).astype(jnp.int32))
    return jnp.where(offset >= 0, forward, backward)


def kernels(shifts, emission, absorption, count):
    grid = jnp.arange(count, dtype=jnp.int32)
    onehot = (shifts[:, None] == grid[None, :]).astype(jnp.float32)
    c_em = jnp.dot(emission, onehot, precision=lax.Precision.HIGHEST)
    c_ab = jnp.dot(absorption, onehot, precision=lax.Precision.HIGHEST)
    return toeplitz(c_em, c_ab, count), toeplitz(c_ab, c_em, count)


def green_parts(energy, level_row, transverse, sig, gam, count, modes):
    width = level_row.shape[0]
    real_part = energy[None, :, None] - level_row[None, None, :] - transverse[:, None, None] - sig[None]
    imag_part = ETA + gam[None]
    denom = real_part * real_part + imag_part * imag_part
    active = (jnp.arange(width, dtype=jnp.int32) < count).astype(jnp.float32)
    g_real = active * real_part / denom
    g_imag = -active * imag_part / denom * jnp.ones_like(real_part)
    shape = (g_real.shape[0], g_real.shape[1], modes, width)
    g_real = jnp.broadcast_to(g_real[:, :, None, :], shape).reshape(-1, width)
    g_imag = jnp.broadcast_to(g_imag[:, :, None, :], shape).reshape(-1, width)
    return g_real, g_imag


def layer_map(prev, src, basis, coupling, g_real, g_imag):
    rows = prev.shape[1]
    width = prev.shape[2]
    x_val = jnp.dot(prev.reshape(2 * rows, width), coupling, preferred_element_type=jnp.float32)
    x_val = (x_val.reshape(2, rows, width) + src.astype(jnp.float32)).astype(jnp.bfloat16)
    y_val = jnp.dot(x_val.reshape(2 * rows, width), basis, preferred_element_type=jnp.float32).reshape(2, rows, width)
    z_val = jnp.stack([y_val[0] * g_real - y_val[1] * g_imag, y_val[0] * g_imag + y_val[1] * g_real]).astype(jnp.bfloat16)
    psi = lax.dot_general(z_val.reshape(2 * rows, width), basis, (((1,), (1,)), ((), ())), preferred_element_type=jnp.float32)
    return psi.reshape(2, rows, width).astype(jnp.bfloat16)


def densities(psi, kcount, ecount, modes, weights, occupation, total):
    width = psi.shape[2]
    values = psi.astype(jnp.float32)
    magnitude = (values[0] * values[0] + values[1] * values[1]).reshape(kcount, ecount, modes, width)
    per_mode = jnp.sum(magnitude * weights[:, None, None, None], axis=0)
    lesser = jnp.einsum("emo,em->eo", per_mode, occupation, precision=lax.Precision.HIGHEST) / total
    greater = jnp.einsum("emo,em->eo", per_mode, 1.0 - occupation, precision=lax.Precision.HIGHEST) / total
    return lesser, greater


def reference(source, basis, coupling, levels, sigma_real, broadening, transverse, counts, occupation, kweight, shifts, emission, absorption):
    energy = energy_grid(ENERGIES)
    k_less, k_great = kernels(shifts, emission, absorption, ENERGIES)
    weights = kweight.astype(jnp.float32)
    total = jnp.sum(kweight).astype(jnp.float32)
    rows = KPTS * ENERGIES * MODES
    prev = jnp.zeros((2, rows, NORB), jnp.bfloat16)
    out_less = []
    out_great = []
    for layer_id in range(LAYERS):
        src = source[layer_id].reshape(2, rows, NORB)
        g_real, g_imag = green_parts(energy, levels[layer_id], transverse, sigma_real[layer_id], broadening[layer_id], counts[layer_id], MODES)
        psi = layer_map(prev, src, basis[layer_id], coupling[layer_id], g_real, g_imag)
        lesser, greater = densities(psi, KPTS, ENERGIES, MODES, weights, occupation, total)
        out_less.append(jnp.dot(k_less, lesser, precision=lax.Precision.HIGHEST).T)
        out_great.append(jnp.dot(k_great, greater, precision=lax.Precision.HIGHEST).T)
        prev = psi
    return jnp.stack(out_less), jnp.stack(out_great)
```

```python
import functools

import jax
import jax.numpy as jnp
from jax import lax
from jax.experimental import pallas as pl
from jax.experimental.pallas import tpu as pltpu
from jax.sharding import PartitionSpec as P

ETA = 1.0
F32 = jnp.float32
BF16 = jnp.bfloat16
VMEM = pltpu.VMEM
SMEM = pltpu.SMEM


def from_behind(shard, axis, by):
    size = lax.axis_size(axis)
    pairs = [(i, i + by) for i in range(size) if 0 <= i + by < size]
    return lax.ppermute(shard, axis, pairs)


def chunk_of(width):
    return 256 if width % 256 == 0 else width


def in_three(value):
    high = value.astype(BF16)
    rest = value - high.astype(F32)
    middle = rest.astype(BF16)
    low = (rest - middle.astype(F32)).astype(BF16)
    return high, middle, low


def write_toeplitz(shifts_ref, emission_ref, absorption_ref, mix_ref):
    count = mix_ref.shape[0]
    points = shifts_ref.shape[1]
    spot = lax.broadcasted_iota(jnp.int32, (2 * count, points), 0)
    shift = shifts_ref[...]
    hit = jnp.where(spot < count, spot, 2 * count - spot) == shift
    onehot = jnp.where(hit, 1.0, 0.0).astype(BF16)
    pieces = in_three(emission_ref[...]) + in_three(absorption_ref[...])
    rows = jnp.concatenate([p.astype(F32) for p in pieces] + [jnp.zeros((2, points), F32)], axis=0)
    sums = lax.dot_general(
        rows.astype(BF16), onehot, (((1,), (1,)), ((), ())), preferred_element_type=F32
    )
    emit = sums[0:1] + sums[1:2] + sums[2:3]
    absorb = sums[3:4] + sums[4:5] + sums[5:6]
    lane = lax.broadcasted_iota(jnp.int32, (1, 2 * count), 1)
    for which, period in enumerate(
        (jnp.where(lane < count, absorb, emit), jnp.where(lane < count, emit, absorb))
    ):
        square = jnp.broadcast_to(period, (count, 2 * count))
        skewed = pltpu.roll(square, 0, 1, stride=1, stride_axis=0)
        mix_ref[:, which * count : (which + 1) * count] = skewed[:, :count]


def strided(ref, tiles, first, count, step):
    return jnp.concatenate([ref[t, pl.ds(first, count, stride=step), :] for t in tiles], axis=1)


def layer_kernel(
    has_prev,
    count_ref,
    trans_hbm,
    kweight_hbm,
    shifts_hbm,
    emission_hbm,
    absorption_hbm,
    levels_hbm,
    sigma_hbm,
    broad_hbm,
    occ_hbm,
    src_hbm,
    basis_hbm,
    *rest,
):
    if has_prev:
        prev_hbm, coupling_hbm, send_ref, mix_ref, psi_ref, *rest, prev_ref, coupling_ref = rest
    else:
        send_ref, mix_ref, *rest = rest
    (
        trans_ref,
        kweight_ref,
        shifts_ref,
        emission_ref,
        absorption_ref,
        levels_ref,
        sigma_ref,
        broad_ref,
        occ_ref,
        src_ref,
        basis_ref,
        g_ref,
        y_ref,
        z_ref,
        sems,
    ) = rest
    kcount, ecount, modes, width = src_ref.shape[2:]
    rows = kcount * ecount * modes
    chunk = chunk_of(width)
    parts = width // chunk
    lanes = y_ref.shape[2]

    pairs = [
        (shifts_hbm, shifts_ref),
        (emission_hbm, emission_ref),
        (absorption_hbm, absorption_ref),
        (trans_hbm, trans_ref),
        (kweight_hbm, kweight_ref),
        (levels_hbm, levels_ref),
        (sigma_hbm, sigma_ref),
        (broad_hbm, broad_ref),
        (occ_hbm, occ_ref),
        (src_hbm, src_ref),
    ]
    for part in range(parts):
        cols = pl.ds(part * chunk, chunk)
        pairs.append((basis_hbm.at[0, :, cols], basis_ref.at[:, cols]))
    if has_prev:
        pairs += [(prev_hbm, prev_ref), (coupling_hbm, coupling_ref)]
    copies = [pltpu.make_async_copy(a, b, sems.at[i]) for i, (a, b) in enumerate(pairs)]
    for copy in copies:
        copy.start()
    for copy in copies[:3]:
        copy.wait()
    write_toeplitz(shifts_ref, emission_ref, absorption_ref, mix_ref)

    for copy in copies[3:9]:
        copy.wait()
    first_energy = lax.axis_index("energy") * ecount
    first_k = lax.axis_index("kpt") * kcount
    energy = (first_energy + lax.broadcasted_iota(jnp.int32, (ecount, 1), 0)).astype(F32)
    energy = (energy + 0.5) * (4.0 / mix_ref.shape[0]) - 2.0
    mode = lax.broadcasted_iota(jnp.int32, (1, width), 1)
    active = jnp.where(mode < count_ref[0], 1.0, 0.0)
    base = energy - levels_ref[...] - sigma_ref[0]
    imag = ETA + broad_ref[0]
    imag2 = imag * imag
    for k in range(kcount):
        real = base - trans_ref[k]
        scale = active / (real * real + imag2)
        g_ref[0, k] = real * scale
        g_ref[1, k] = -imag * scale

    copies[9].wait()
    x_val = src_ref[0].reshape(2 * rows, width)
    if has_prev:
        copies[10 + parts].wait()
        copies[11 + parts].wait()
        carried = jnp.dot(
            prev_ref[...], coupling_ref[0], preferred_element_type=F32
        )
        x_val = (carried + x_val.astype(F32)).astype(BF16)
    for part in range(parts):
        cols = pl.ds(part * chunk, chunk)
        copies[10 + part].wait()
        y_val = jnp.dot(x_val, basis_ref[:, cols], preferred_element_type=F32)
        for t in range(chunk // lanes):
            y_ref[part * (chunk // lanes) + t] = y_val[:, t * lanes : (t + 1) * lanes]
        tiles = range(part * (chunk // lanes), (part + 1) * (chunk // lanes))
        for k in range(kcount):
            g_real = g_ref[0, k, :, cols]
            g_imag = g_ref[1, k, :, cols]
            z_re = []
            z_im = []
            for m in range(modes):
                first = k * ecount * modes + m
                y_re = strided(y_ref, tiles, first, ecount, modes)
                y_im = strided(y_ref, tiles, rows + first, ecount, modes)
                z_re.append(y_re * g_real - y_im * g_imag)
                z_im.append(y_re * g_imag + y_im * g_real)
            group = pl.ds(k * ecount * modes, ecount * modes)
            z_ref[group, cols] = jnp.concatenate(z_re, axis=0).astype(BF16)
            group = pl.ds(rows + k * ecount * modes, ecount * modes)
            z_ref[group, cols] = jnp.concatenate(z_im, axis=0).astype(BF16)

    total = kweight_ref[0]
    for k in range(1, kweight_ref.shape[0]):
        total = total + kweight_ref[k]
    total = jnp.full((ecount, 1), total, jnp.int32).astype(F32)
    weights = [kweight_ref[first_k + k].astype(F32) for k in range(kcount)]
    diagonal = lax.broadcasted_iota(jnp.int32, (ecount, ecount), 0) == lax.broadcasted_iota(
        jnp.int32, (ecount, ecount), 1
    )
    filled = []
    for m in range(modes):
        row = jnp.broadcast_to(occ_ref[m : m + 1, :], (ecount, ecount))
        filled.append(jnp.sum(jnp.where(diagonal, row, 0.0), axis=1, keepdims=True))
    less_of = [f / total for f in filled]
    great_of = [(1.0 - f) / total for f in filled]

    targets = send_ref.shape[0]
    copies_k = send_ref.shape[1]
    block = width // targets
    for part in range(parts):
        psi = lax.dot_general(
            z_ref[...],
            basis_ref[pl.ds(part * chunk, chunk), :],
            (((1,), (1,)), ((), ())),
            preferred_element_type=F32,
        )
        if has_prev:
            psi_ref[:, pl.ds(part * chunk, chunk)] = psi.astype(BF16)
        less = None
        great = None
        for m in range(modes):
            per_mode = None
            for k in range(kcount):
                first = (k * modes + m) * ecount
                re = psi[first : first + ecount]
                im = psi[rows + first : rows + first + ecount]
                term = (re * re + im * im) * weights[k]
                per_mode = term if per_mode is None else per_mode + term
            less = per_mode * less_of[m] if less is None else less + per_mode * less_of[m]
            great = per_mode * great_of[m] if great is None else great + per_mode * great_of[m]
        for t in range(chunk // block):
            both = jnp.concatenate(
                [less[:, t * block : (t + 1) * block], great[:, t * block : (t + 1) * block]], axis=1
            ).astype(BF16)
            for c in range(copies_k):
                send_ref[part * (chunk // block) + t, c] = both


def mix_kernel(got_ref, mix_ref, less_ref, great_ref):
    count = mix_ref.shape[0]
    got = got_ref[...].astype(F32)
    dens = jnp.sum(got, axis=1).reshape(count, got.shape[3])
    out = lax.dot_general(
        dens,
        mix_ref[...],
        (((0,), (0,)), ((), ())),
        precision=lax.Precision.HIGHEST,
        preferred_element_type=F32,
    )
    block = less_ref.shape[1]
    less_ref[0] = out[:block, :count]
    great_ref[0] = out[block:, count:]


def on_device(
    source,
    basis,
    coupling,
    levels,
    sigma_real,
    broadening,
    transverse,
    counts,
    occupation,
    kweight,
    shifts,
    emission,
    absorption,
):
    kcount, ecount, modes, width = source.shape[2:]
    rows = kcount * ecount * modes
    energy_devs = lax.axis_size("energy")
    k_devs = lax.axis_size("kpt")
    layer_devs = lax.axis_size("layer")
    all_energies = ecount * energy_devs
    block = width // energy_devs
    parts = width // chunk_of(width)
    vmem = pl.BlockSpec(memory_space=VMEM)
    hbm = pl.BlockSpec(memory_space=pltpu.HBM)
    operands = (
        counts,
        transverse,
        kweight,
        shifts[None],
        emission[None],
        absorption[None],
        levels,
        sigma_real,
        broadening,
        occupation.T,
        source,
        basis,
    )
    send_shape = jax.ShapeDtypeStruct((energy_devs, k_devs, ecount, 2 * block), BF16)
    mix_shape = jax.ShapeDtypeStruct((all_energies, 2 * all_energies), F32)
    scratch = (
        [SMEM(a.shape, a.dtype) for a in operands[1:3]]
        + [VMEM(a.shape, a.dtype) for a in operands[3:11]]
        + [
            VMEM((width, width), BF16),
            VMEM((2, kcount, ecount, width), F32),
            VMEM((width // 128, 2 * rows, 128), F32),
            VMEM((2 * rows, width), BF16),
        ]
    )
    psi_shape = jax.ShapeDtypeStruct((2 * rows, width), BF16)

    def layer(prev):
        has_prev = prev is not None
        more = (prev, coupling) if has_prev else ()
        in_hbm = [pltpu.with_memory_space_constraint(a, pltpu.HBM) for a in operands[1:] + more]
        sems = pltpu.SemaphoreType.DMA((10 + parts + len(more),))
        return pl.pallas_call(
            functools.partial(layer_kernel, has_prev),
            out_shape=(send_shape, mix_shape) + ((psi_shape,) if has_prev else ()),
            in_specs=[pl.BlockSpec(memory_space=SMEM)] + [hbm] * len(in_hbm),
            out_specs=(vmem,) * (3 if has_prev else 2),
            scratch_shapes=scratch + [sems] + [VMEM(a.shape, a.dtype) for a in more],
            compiler_params=pltpu.CompilerParams(vmem_limit_bytes=24 * 1024 * 1024),
        )(operands[0], *in_hbm)

    if layer_devs == 1:
        send, mix = layer(None)
    else:
        layer_pos = lax.axis_index("layer")

        def sweep(step, state):
            carry, kept = state
            kept = lax.cond(step == layer_pos, lambda: tuple(layer(carry)), lambda: kept)
            carry = kept[2].reshape(2, kcount, modes, ecount, width).transpose(0, 1, 3, 2, 4)
            carry = from_behind(carry.reshape(2 * rows, width), "layer", 1)
            return carry, kept

        stored = tuple(jnp.zeros(a.shape, a.dtype) for a in (send_shape, mix_shape, psi_shape))
        send, mix, _ = lax.fori_loop(0, layer_devs, sweep, (stored[2], stored))[1]
    got = lax.all_to_all(
        send.reshape(energy_devs * k_devs, ecount, 2 * block), ("energy", "kpt"), 0, 0, tiled=True
    ).reshape(energy_devs, k_devs, ecount, 2 * block)
    out_shape = jax.ShapeDtypeStruct((1, block, all_energies), F32)
    return pl.pallas_call(
        mix_kernel,
        out_shape=(out_shape, out_shape),
        in_specs=[vmem, vmem],
        out_specs=(vmem, vmem),
        compiler_params=pltpu.CompilerParams(vmem_limit_bytes=8 * 1024 * 1024),
    )(got, mix)


def solution(mesh):
    in_specs = (
        P("layer", None, "kpt", "energy", None, None),
        P("layer", None, None),
        P("layer", None, None),
        P("layer", None),
        P("layer", "energy", None),
        P("layer", "energy", None),
        P("kpt"),
        P("layer"),
        P("energy", None),
        P(),
        P(),
        P(),
        P(),
    )
    out_specs = (P("layer", "energy", None), P("layer", "energy", None))
    return jax.shard_map(
        on_device, mesh=mesh, in_specs=in_specs, out_specs=out_specs, check_vma=False
    )
```

```python
import functools

import jax
import jax.numpy as jnp
from jax import lax
from jax.experimental import pallas as pl
from jax.experimental.pallas import tpu as pltpu
from jax.sharding import PartitionSpec as P

ETA = 1.0
F32 = jnp.float32
BF16 = jnp.bfloat16
VMEM = pltpu.VMEM
SMEM = pltpu.SMEM


def from_behind(shard, axis, by):
    size = lax.axis_size(axis)
    pairs = [(i, i + by) for i in range(size) if 0 <= i + by < size]
    return lax.ppermute(shard, axis, pairs)


def chunk_of(width):
    return 256 if width % 256 == 0 else width


def in_three(value):
    high = value.astype(BF16)
    rest = value - high.astype(F32)
    middle = rest.astype(BF16)
    low = (rest - middle.astype(F32)).astype(BF16)
    return high, middle, low


def write_toeplitz(shifts_ref, emission_ref, absorption_ref, mix_ref):
    count = mix_ref.shape[0]
    points = shifts_ref.shape[1]
    spot = lax.broadcasted_iota(jnp.int32, (2 * count, points), 0)
    shift = shifts_ref[...]
    hit = jnp.where(spot < count, spot, 2 * count - spot) == shift
    onehot = jnp.where(hit, 1.0, 0.0).astype(BF16)
    pieces = in_three(emission_ref[...]) + in_three(absorption_ref[...])
    rows = jnp.concatenate([p.astype(F32) for p in pieces] + [jnp.zeros((2, points), F32)], axis=0)
    sums = lax.dot_general(
        rows.astype(BF16), onehot, (((1,), (1,)), ((), ())), preferred_element_type=F32
    )
    emit = sums[0:1] + sums[1:2] + sums[2:3]
    absorb = sums[3:4] + sums[4:5] + sums[5:6]
    lane = lax.broadcasted_iota(jnp.int32, (1, 2 * count), 1)
    for which, period in enumerate(
        (jnp.where(lane < count, absorb, emit), jnp.where(lane < count, emit, absorb))
    ):
        square = jnp.broadcast_to(period, (count, 2 * count))
        skewed = pltpu.roll(square, 0, 1, stride=1, stride_axis=0)
        mix_ref[:, which * count : (which + 1) * count] = skewed[:, :count]


def strided(ref, tiles, first, count, step):
    return jnp.concatenate([ref[t, pl.ds(first, count, stride=step), :] for t in tiles], axis=1)


def layer_kernel(
    has_prev,
    count_ref,
    trans_hbm,
    kweight_hbm,
    shifts_hbm,
    emission_hbm,
    absorption_hbm,
    levels_hbm,
    sigma_hbm,
    broad_hbm,
    occ_hbm,
    src_hbm,
    basis_hbm,
    *rest,
):
    if has_prev:
        prev_hbm, coupling_hbm, send_ref, mix_ref, psi_ref, *rest, prev_ref, coupling_ref = rest
    else:
        send_ref, mix_ref, *rest = rest
    (
        trans_ref,
        kweight_ref,
        shifts_ref,
        emission_ref,
        absorption_ref,
        levels_ref,
        sigma_ref,
        broad_ref,
        occ_ref,
        src_ref,
        basis_ref,
        g_ref,
        y_ref,
        z_ref,
        x_ref,
        sems,
    ) = rest
    kcount, ecount, modes, width = src_ref.shape[2:]
    rows = kcount * ecount * modes
    chunk = chunk_of(width)
    parts = width // chunk
    lanes = y_ref.shape[2]

    pairs = [
        (shifts_hbm, shifts_ref),
        (emission_hbm, emission_ref),
        (absorption_hbm, absorption_ref),
        (trans_hbm, trans_ref),
        (kweight_hbm, kweight_ref),
        (levels_hbm, levels_ref),
        (sigma_hbm, sigma_ref),
        (broad_hbm, broad_ref),
        (occ_hbm, occ_ref),
        (src_hbm, src_ref),
    ]
    for part in range(parts):
        cols = pl.ds(part * chunk, chunk)
        pairs.append((basis_hbm.at[0, cols, :], basis_ref.at[cols, :]))
    if has_prev:
        pairs += [(prev_hbm, prev_ref), (coupling_hbm, coupling_ref)]
    copies = [pltpu.make_async_copy(a, b, sems.at[i]) for i, (a, b) in enumerate(pairs)]
    small, carried, wide = copies[:9], copies[10 + parts :], copies[9 : 10 + parts]
    for copy in small + wide + carried:
        copy.start()
    for copy in small:
        copy.wait()
    first_energy = lax.axis_index("energy") * ecount
    first_k = lax.axis_index("kpt") * kcount
    energy = (first_energy + lax.broadcasted_iota(jnp.int32, (ecount, 1), 0)).astype(F32)
    energy = (energy + 0.5) * (4.0 / mix_ref.shape[0]) - 2.0
    mode = lax.broadcasted_iota(jnp.int32, (1, width), 1)
    active = jnp.where(mode < count_ref[0], 1.0, 0.0)
    base = energy - levels_ref[...] - sigma_ref[0]
    imag = ETA + broad_ref[0]
    imag2 = imag * imag
    for k in range(kcount):
        real = base - trans_ref[k]
        scale = active / (real * real + imag2)
        g_ref[0, k] = real * scale
        g_ref[1, k] = -imag * scale
    write_toeplitz(shifts_ref, emission_ref, absorption_ref, mix_ref)

    total = kweight_ref[0]
    for k in range(1, kweight_ref.shape[0]):
        total = total + kweight_ref[k]
    total = jnp.full((ecount, 1), total, jnp.int32).astype(F32)
    weights = [kweight_ref[first_k + k].astype(F32) for k in range(kcount)]
    diagonal = lax.broadcasted_iota(jnp.int32, (ecount, ecount), 0) == lax.broadcasted_iota(
        jnp.int32, (ecount, ecount), 1
    )
    filled = []
    for m in range(modes):
        row = jnp.broadcast_to(occ_ref[m : m + 1, :], (ecount, ecount))
        filled.append(jnp.sum(jnp.where(diagonal, row, 0.0), axis=1, keepdims=True))
    less_of = [f / total for f in filled]
    great_of = [(1.0 - f) / total for f in filled]

    def scale_modes(part):
        cols = pl.ds(part * chunk, chunk)
        tiles = range(part * (chunk // lanes), (part + 1) * (chunk // lanes))
        for k in range(kcount):
            g_real = g_ref[0, k, :, cols]
            g_imag = g_ref[1, k, :, cols]
            z_re = []
            z_im = []
            for m in range(modes):
                first = k * ecount * modes + m
                y_re = strided(y_ref, tiles, first, ecount, modes)
                y_im = strided(y_ref, tiles, rows + first, ecount, modes)
                z_re.append(y_re * g_real - y_im * g_imag)
                z_im.append(y_re * g_imag + y_im * g_real)
            group = pl.ds(k * ecount * modes, ecount * modes)
            z_ref[group, cols] = jnp.concatenate(z_re, axis=0).astype(BF16)
            group = pl.ds(rows + k * ecount * modes, ecount * modes)
            z_ref[group, cols] = jnp.concatenate(z_im, axis=0).astype(BF16)

    copies_k = send_ref.shape[1]
    block = width // send_ref.shape[0]

    def densities(part, psi):
        if has_prev:
            psi_ref[:, pl.ds(part * chunk, chunk)] = psi.astype(BF16)
        less = None
        great = None
        for m in range(modes):
            per_mode = None
            for k in range(kcount):
                first = (k * modes + m) * ecount
                re = psi[first : first + ecount]
                im = psi[rows + first : rows + first + ecount]
                term = (re * re + im * im) * weights[k]
                per_mode = term if per_mode is None else per_mode + term
            less = per_mode * less_of[m] if less is None else less + per_mode * less_of[m]
            great = per_mode * great_of[m] if great is None else great + per_mode * great_of[m]
        for t in range(chunk // block):
            both = jnp.concatenate(
                [less[:, t * block : (t + 1) * block], great[:, t * block : (t + 1) * block]], axis=1
            ).astype(BF16)
            for c in range(copies_k):
                send_ref[part * (chunk // block) + t, c] = both

    wide[0].wait()
    x_ref[...] = src_ref[0].reshape(2 * rows, width)
    if has_prev:
        for copy in carried:
            copy.wait()
        brought = jnp.dot(prev_ref[...], coupling_ref[0], preferred_element_type=F32)
        x_ref[...] = (brought + x_ref[...].astype(F32)).astype(BF16)
    stages = min(2, parts)
    for stage in range(stages):
        first_part = stage * parts // stages
        last_part = (stage + 1) * parts // stages
        for part in range(first_part, last_part):
            wide[1 + part].wait()
        depth = pl.ds(first_part * chunk, (last_part - first_part) * chunk)
        for part in range(parts):
            cols = pl.ds(part * chunk, chunk)
            y_val = jnp.dot(x_ref[:, depth], basis_ref[depth, cols], preferred_element_type=F32)
            for t in range(chunk // lanes):
                tile = part * (chunk // lanes) + t
                piece = y_val[:, t * lanes : (t + 1) * lanes]
                y_ref[tile] = piece if stage == 0 else y_ref[tile] + piece
    for part in range(parts):
        scale_modes(part)
    for part in range(parts):
        psi = lax.dot_general(
            z_ref[...],
            basis_ref[pl.ds(part * chunk, chunk), :],
            (((1,), (1,)), ((), ())),
            preferred_element_type=F32,
        )
        densities(part, psi)


def mix_kernel(got_ref, mix_ref, less_ref, great_ref):
    count = mix_ref.shape[0]
    got = got_ref[...].astype(F32)
    dens = jnp.sum(got, axis=1).reshape(count, got.shape[3])
    out = lax.dot_general(
        dens,
        mix_ref[...],
        (((0,), (0,)), ((), ())),
        precision=lax.Precision.HIGHEST,
        preferred_element_type=F32,
    )
    block = less_ref.shape[1]
    less_ref[0] = out[:block, :count]
    great_ref[0] = out[block:, count:]


def on_device(
    source,
    basis,
    coupling,
    levels,
    sigma_real,
    broadening,
    transverse,
    counts,
    occupation,
    kweight,
    shifts,
    emission,
    absorption,
):
    kcount, ecount, modes, width = source.shape[2:]
    rows = kcount * ecount * modes
    energy_devs = lax.axis_size("energy")
    k_devs = lax.axis_size("kpt")
    layer_devs = lax.axis_size("layer")
    all_energies = ecount * energy_devs
    block = width // energy_devs
    parts = width // chunk_of(width)
    vmem = pl.BlockSpec(memory_space=VMEM)
    hbm = pl.BlockSpec(memory_space=pltpu.HBM)
    operands = (
        counts,
        transverse,
        kweight,
        shifts[None],
        emission[None],
        absorption[None],
        levels,
        sigma_real,
        broadening,
        occupation.T,
        source,
        basis,
    )
    send_shape = jax.ShapeDtypeStruct((energy_devs, k_devs, ecount, 2 * block), BF16)
    mix_shape = jax.ShapeDtypeStruct((all_energies, 2 * all_energies), F32)
    scratch = (
        [SMEM(a.shape, a.dtype) for a in operands[1:3]]
        + [VMEM(a.shape, a.dtype) for a in operands[3:11]]
        + [
            VMEM((width, width), BF16),
            VMEM((2, kcount, ecount, width), F32),
            VMEM((width // 128, 2 * rows, 128), F32),
            VMEM((2 * rows, width), BF16),
            VMEM((2 * rows, width), BF16),
        ]
    )
    psi_shape = jax.ShapeDtypeStruct((2 * rows, width), BF16)

    def layer(prev):
        has_prev = prev is not None
        more = (prev, coupling) if has_prev else ()
        in_hbm = [pltpu.with_memory_space_constraint(a, pltpu.HBM) for a in operands[1:] + more]
        sems = pltpu.SemaphoreType.DMA((10 + parts + len(more),))
        return pl.pallas_call(
            functools.partial(layer_kernel, has_prev),
            out_shape=(send_shape, mix_shape) + ((psi_shape,) if has_prev else ()),
            in_specs=[pl.BlockSpec(memory_space=SMEM)] + [hbm] * len(in_hbm),
            out_specs=(vmem,) * (3 if has_prev else 2),
            scratch_shapes=scratch + [sems] + [VMEM(a.shape, a.dtype) for a in more],
            compiler_params=pltpu.CompilerParams(vmem_limit_bytes=24 * 1024 * 1024),
        )(operands[0], *in_hbm)

    if layer_devs == 1:
        send, mix = layer(None)
    else:
        layer_pos = lax.axis_index("layer")

        def sweep(step, state):
            carry, kept = state
            kept = lax.cond(step == layer_pos, lambda: tuple(layer(carry)), lambda: kept)
            carry = kept[2].reshape(2, kcount, modes, ecount, width).transpose(0, 1, 3, 2, 4)
            carry = from_behind(carry.reshape(2 * rows, width), "layer", 1)
            return carry, kept

        stored = tuple(jnp.zeros(a.shape, a.dtype) for a in (send_shape, mix_shape, psi_shape))
        send, mix, _ = lax.fori_loop(0, layer_devs, sweep, (stored[2], stored))[1]
    got = lax.all_to_all(
        send.reshape(energy_devs * k_devs, ecount, 2 * block), ("energy", "kpt"), 0, 0, tiled=True
    ).reshape(energy_devs, k_devs, ecount, 2 * block)
    out_shape = jax.ShapeDtypeStruct((1, block, all_energies), F32)
    return pl.pallas_call(
        mix_kernel,
        out_shape=(out_shape, out_shape),
        in_specs=[vmem, vmem],
        out_specs=(vmem, vmem),
        compiler_params=pltpu.CompilerParams(vmem_limit_bytes=8 * 1024 * 1024),
    )(got, mix)


def solution(mesh):
    in_specs = (
        P("layer", None, "kpt", "energy", None, None),
        P("layer", None, None),
        P("layer", None, None),
        P("layer", None),
        P("layer", "energy", None),
        P("layer", "energy", None),
        P("kpt"),
        P("layer"),
        P("energy", None),
        P(),
        P(),
        P(),
        P(),
    )
    out_specs = (P("layer", "energy", None), P("layer", "energy", None))
    return jax.shard_map(
        on_device, mesh=mesh, in_specs=in_specs, out_specs=out_specs, check_vma=False
    )
```

```python
import functools

import jax
import jax.numpy as jnp
from jax import lax
from jax.experimental import pallas as pl
from jax.experimental.pallas import tpu as pltpu
from jax.sharding import PartitionSpec as P

ETA = 1.0
F32 = jnp.float32
BF16 = jnp.bfloat16
VMEM = pltpu.VMEM
SMEM = pltpu.SMEM


def from_behind(shard, axis, by):
    size = lax.axis_size(axis)
    pairs = [(i, i + by) for i in range(size) if 0 <= i + by < size]
    return lax.ppermute(shard, axis, pairs)


def chunk_of(width):
    return 256 if width % 256 == 0 else width


def in_three(value):
    high = value.astype(BF16)
    rest = value - high.astype(F32)
    middle = rest.astype(BF16)
    low = (rest - middle.astype(F32)).astype(BF16)
    return high, middle, low


def write_toeplitz(shifts_ref, emission_ref, absorption_ref, mix_ref, energy_devs, k_devs):
    count = mix_ref.shape[1] // 4
    points = shifts_ref.shape[1]
    spot = lax.broadcasted_iota(jnp.int32, (2 * count, points), 0)
    shift = shifts_ref[...]
    hit = jnp.where(spot < count, spot, 2 * count - spot) == shift
    onehot = jnp.where(hit, 1.0, 0.0).astype(BF16)
    pieces = in_three(emission_ref[...]) + in_three(absorption_ref[...])
    rows = jnp.concatenate([p.astype(F32) for p in pieces] + [jnp.zeros((2, points), F32)], axis=0)
    sums = lax.dot_general(
        rows.astype(BF16), onehot, (((1,), (1,)), ((), ())), preferred_element_type=F32
    )
    emit = sums[0:1] + sums[1:2] + sums[2:3]
    absorb = sums[3:4] + sums[4:5] + sums[5:6]
    lane = lax.broadcasted_iota(jnp.int32, (1, 2 * count), 1)
    for which, period in enumerate(
        (jnp.where(lane < count, absorb, emit), jnp.where(lane < count, emit, absorb))
    ):
        square = jnp.broadcast_to(period, (count, 2 * count))
        skewed = pltpu.roll(square, 0, 1, stride=1, stride_axis=0)[:, :count]
        high = skewed.astype(BF16).astype(F32)
        for side, piece in enumerate((high, skewed - high)):
            blocks = piece.reshape(energy_devs, 1, count // energy_devs, count)
            blocks = jnp.broadcast_to(
                blocks, (energy_devs, k_devs, count // energy_devs, count)
            ).reshape(k_devs * count, count)
            first = (2 * side + which) * count
            mix_ref[:, first : first + count] = blocks.astype(BF16)


def strided(ref, tiles, first, count, step):
    return jnp.concatenate([ref[t, pl.ds(first, count, stride=step), :] for t in tiles], axis=1)


def layer_kernel(
    has_prev,
    count_ref,
    trans_hbm,
    kweight_hbm,
    shifts_hbm,
    emission_hbm,
    absorption_hbm,
    levels_hbm,
    sigma_hbm,
    broad_hbm,
    occ_hbm,
    src_hbm,
    basis_hbm,
    *rest,
):
    if has_prev:
        prev_hbm, coupling_hbm, send_ref, mix_ref, psi_ref, *rest, prev_ref, coupling_ref = rest
    else:
        send_ref, mix_ref, *rest = rest
    (
        trans_ref,
        kweight_ref,
        shifts_ref,
        emission_ref,
        absorption_ref,
        levels_ref,
        sigma_ref,
        broad_ref,
        occ_ref,
        src_ref,
        basis_ref,
        g_ref,
        y_ref,
        z_ref,
        x_ref,
        sems,
    ) = rest
    kcount, ecount, modes, width = src_ref.shape[2:]
    rows = kcount * ecount * modes
    chunk = chunk_of(width)
    parts = width // chunk
    lanes = y_ref.shape[2]

    pairs = [
        (shifts_hbm, shifts_ref),
        (emission_hbm, emission_ref),
        (absorption_hbm, absorption_ref),
        (trans_hbm, trans_ref),
        (kweight_hbm, kweight_ref),
        (levels_hbm, levels_ref),
        (sigma_hbm, sigma_ref),
        (broad_hbm, broad_ref),
        (occ_hbm, occ_ref),
        (src_hbm, src_ref),
    ]
    for part in range(parts):
        cols = pl.ds(part * chunk, chunk)
        pairs.append((basis_hbm.at[0, cols, :], basis_ref.at[cols, :]))
    if has_prev:
        pairs += [(prev_hbm, prev_ref), (coupling_hbm, coupling_ref)]
    copies = [pltpu.make_async_copy(a, b, sems.at[i]) for i, (a, b) in enumerate(pairs)]
    small, carried, wide = copies[:9], copies[10 + parts :], copies[9 : 10 + parts]
    for copy in small + wide + carried:
        copy.start()
    for copy in small:
        copy.wait()
    first_energy = lax.axis_index("energy") * ecount
    first_k = lax.axis_index("kpt") * kcount
    energy = (first_energy + lax.broadcasted_iota(jnp.int32, (ecount, 1), 0)).astype(F32)
    energy = (energy + 0.5) * (4.0 / (mix_ref.shape[1] // 4)) - 2.0
    mode = lax.broadcasted_iota(jnp.int32, (1, width), 1)
    active = jnp.where(mode < count_ref[0], 1.0, 0.0)
    base = energy - levels_ref[...] - sigma_ref[0]
    imag = ETA + broad_ref[0]
    imag2 = imag * imag
    for k in range(kcount):
        real = base - trans_ref[k]
        scale = active / (real * real + imag2)
        g_ref[0, k] = real * scale
        g_ref[1, k] = -imag * scale
    write_toeplitz(shifts_ref, emission_ref, absorption_ref, mix_ref, *send_ref.shape[:2])

    total = kweight_ref[0]
    for k in range(1, kweight_ref.shape[0]):
        total = total + kweight_ref[k]
    total = jnp.full((ecount, 1), total, jnp.int32).astype(F32)
    weights = [kweight_ref[first_k + k].astype(F32) for k in range(kcount)]
    diagonal = lax.broadcasted_iota(jnp.int32, (ecount, ecount), 0) == lax.broadcasted_iota(
        jnp.int32, (ecount, ecount), 1
    )
    filled = []
    for m in range(modes):
        row = jnp.broadcast_to(occ_ref[m : m + 1, :], (ecount, ecount))
        filled.append(jnp.sum(jnp.where(diagonal, row, 0.0), axis=1, keepdims=True))
    less_of = [f / total for f in filled]
    great_of = [(1.0 - f) / total for f in filled]

    def scale_modes(part):
        cols = pl.ds(part * chunk, chunk)
        tiles = range(part * (chunk // lanes), (part + 1) * (chunk // lanes))
        for k in range(kcount):
            g_real = g_ref[0, k, :, cols]
            g_imag = g_ref[1, k, :, cols]
            z_re = []
            z_im = []
            for m in range(modes):
                first = k * ecount * modes + m
                y_re = strided(y_ref, tiles, first, ecount, modes)
                y_im = strided(y_ref, tiles, rows + first, ecount, modes)
                z_re.append(y_re * g_real - y_im * g_imag)
                z_im.append(y_re * g_imag + y_im * g_real)
            group = pl.ds(k * ecount * modes, ecount * modes)
            z_ref[group, cols] = jnp.concatenate(z_re, axis=0).astype(BF16)
            group = pl.ds(rows + k * ecount * modes, ecount * modes)
            z_ref[group, cols] = jnp.concatenate(z_im, axis=0).astype(BF16)

    copies_k = send_ref.shape[1]
    block = width // send_ref.shape[0]

    def densities(part, psi):
        if has_prev:
            psi_ref[:, pl.ds(part * chunk, chunk)] = psi.astype(BF16)
        less = None
        great = None
        for m in range(modes):
            per_mode = None
            for k in range(kcount):
                first = (k * modes + m) * ecount
                re = psi[first : first + ecount]
                im = psi[rows + first : rows + first + ecount]
                term = (re * re + im * im) * weights[k]
                per_mode = term if per_mode is None else per_mode + term
            less = per_mode * less_of[m] if less is None else less + per_mode * less_of[m]
            great = per_mode * great_of[m] if great is None else great + per_mode * great_of[m]
        for t in range(chunk // block):
            both = jnp.concatenate(
                [less[:, t * block : (t + 1) * block], great[:, t * block : (t + 1) * block]], axis=1
            ).astype(BF16)
            for c in range(copies_k):
                send_ref[part * (chunk // block) + t, c] = both

    wide[0].wait()
    x_ref[...] = src_ref[0].reshape(2 * rows, width)
    if has_prev:
        for copy in carried:
            copy.wait()
        brought = jnp.dot(prev_ref[...], coupling_ref[0], preferred_element_type=F32)
        x_ref[...] = (brought + x_ref[...].astype(F32)).astype(BF16)
    stages = min(2, parts)
    for stage in range(stages):
        first_part = stage * parts // stages
        last_part = (stage + 1) * parts // stages
        for part in range(first_part, last_part):
            wide[1 + part].wait()
        depth = pl.ds(first_part * chunk, (last_part - first_part) * chunk)
        for part in range(parts):
            cols = pl.ds(part * chunk, chunk)
            y_val = jnp.dot(x_ref[:, depth], basis_ref[depth, cols], preferred_element_type=F32)
            for t in range(chunk // lanes):
                tile = part * (chunk // lanes) + t
                piece = y_val[:, t * lanes : (t + 1) * lanes]
                y_ref[tile] = piece if stage == 0 else y_ref[tile] + piece
    for part in range(parts):
        scale_modes(part)
    for part in range(parts):
        psi = lax.dot_general(
            z_ref[...],
            basis_ref[pl.ds(part * chunk, chunk), :],
            (((1,), (1,)), ((), ())),
            preferred_element_type=F32,
        )
        densities(part, psi)


def mix_kernel(got_ref, mix_ref, less_ref, great_ref):
    depth = mix_ref.shape[0]
    count = mix_ref.shape[1] // 4
    dens = got_ref[...].astype(F32).reshape(depth, got_ref.shape[3]).astype(BF16)
    out = lax.dot_general(
        dens, mix_ref[...], (((0,), (0,)), ((), ())), preferred_element_type=F32
    )
    out = out[:, : 2 * count] + out[:, 2 * count :]
    block = less_ref.shape[1]
    less_ref[0] = out[:block, :count]
    great_ref[0] = out[block:, count:]


def on_device(
    source,
    basis,
    coupling,
    levels,
    sigma_real,
    broadening,
    transverse,
    counts,
    occupation,
    kweight,
    shifts,
    emission,
    absorption,
):
    kcount, ecount, modes, width = source.shape[2:]
    rows = kcount * ecount * modes
    energy_devs = lax.axis_size("energy")
    k_devs = lax.axis_size("kpt")
    layer_devs = lax.axis_size("layer")
    all_energies = ecount * energy_devs
    block = width // energy_devs
    parts = width // chunk_of(width)
    vmem = pl.BlockSpec(memory_space=VMEM)
    hbm = pl.BlockSpec(memory_space=pltpu.HBM)
    operands = (
        counts,
        transverse,
        kweight,
        shifts[None],
        emission[None],
        absorption[None],
        levels,
        sigma_real,
        broadening,
        occupation.T,
        source,
        basis,
    )
    send_shape = jax.ShapeDtypeStruct((energy_devs, k_devs, ecount, 2 * block), BF16)
    mix_shape = jax.ShapeDtypeStruct((k_devs * all_energies, 4 * all_energies), BF16)
    scratch = (
        [SMEM(a.shape, a.dtype) for a in operands[1:3]]
        + [VMEM(a.shape, a.dtype) for a in operands[3:11]]
        + [
            VMEM((width, width), BF16),
            VMEM((2, kcount, ecount, width), F32),
            VMEM((width // 128, 2 * rows, 128), F32),
            VMEM((2 * rows, width), BF16),
            VMEM((2 * rows, width), BF16),
        ]
    )
    psi_shape = jax.ShapeDtypeStruct((2 * rows, width), BF16)

    def layer(prev):
        has_prev = prev is not None
        more = (prev, coupling) if has_prev else ()
        in_hbm = [pltpu.with_memory_space_constraint(a, pltpu.HBM) for a in operands[1:] + more]
        sems = pltpu.SemaphoreType.DMA((10 + parts + len(more),))
        return pl.pallas_call(
            functools.partial(layer_kernel, has_prev),
            out_shape=(send_shape, mix_shape) + ((psi_shape,) if has_prev else ()),
            in_specs=[pl.BlockSpec(memory_space=SMEM)] + [hbm] * len(in_hbm),
            out_specs=(vmem,) * (3 if has_prev else 2),
            scratch_shapes=scratch + [sems] + [VMEM(a.shape, a.dtype) for a in more],
            compiler_params=pltpu.CompilerParams(vmem_limit_bytes=24 * 1024 * 1024),
        )(operands[0], *in_hbm)

    if layer_devs == 1:
        send, mix = layer(None)
    else:
        layer_pos = lax.axis_index("layer")

        def sweep(step, state):
            carry, kept = state
            kept = lax.cond(step == layer_pos, lambda: tuple(layer(carry)), lambda: kept)
            carry = kept[2].reshape(2, kcount, modes, ecount, width).transpose(0, 1, 3, 2, 4)
            carry = from_behind(carry.reshape(2 * rows, width), "layer", 1)
            return carry, kept

        stored = tuple(jnp.zeros(a.shape, a.dtype) for a in (send_shape, mix_shape, psi_shape))
        send, mix, _ = lax.fori_loop(0, layer_devs, sweep, (stored[2], stored))[1]
    got = lax.all_to_all(
        send.reshape(energy_devs * k_devs, ecount, 2 * block), ("energy", "kpt"), 0, 0, tiled=True
    ).reshape(energy_devs, k_devs, ecount, 2 * block)
    out_shape = jax.ShapeDtypeStruct((1, block, all_energies), F32)
    return pl.pallas_call(
        mix_kernel,
        out_shape=(out_shape, out_shape),
        in_specs=[vmem, vmem],
        out_specs=(vmem, vmem),
        compiler_params=pltpu.CompilerParams(vmem_limit_bytes=8 * 1024 * 1024),
    )(got, mix)


def solution(mesh):
    in_specs = (
        P("layer", None, "kpt", "energy", None, None),
        P("layer", None, None),
        P("layer", None, None),
        P("layer", None),
        P("layer", "energy", None),
        P("layer", "energy", None),
        P("kpt"),
        P("layer"),
        P("energy", None),
        P(),
        P(),
        P(),
        P(),
    )
    out_specs = (P("layer", "energy", None), P("layer", "energy", None))
    return jax.shard_map(
        on_device, mesh=mesh, in_specs=in_specs, out_specs=out_specs, check_vma=False
    )
```

```python
import functools

import jax
import jax.numpy as jnp
from jax import lax
from jax.experimental import pallas as pl
from jax.experimental.pallas import tpu as pltpu
from jax.sharding import PartitionSpec as P

ETA = 1.0
F32 = jnp.float32
BF16 = jnp.bfloat16
VMEM = pltpu.VMEM
SMEM = pltpu.SMEM


def from_behind(shard, axis, by):
    size = lax.axis_size(axis)
    pairs = [(i, i + by) for i in range(size) if 0 <= i + by < size]
    return lax.ppermute(shard, axis, pairs)


def chunk_of(width):
    return 256 if width % 256 == 0 else width


def in_three(value):
    high = value.astype(BF16)
    rest = value - high.astype(F32)
    middle = rest.astype(BF16)
    low = (rest - middle.astype(F32)).astype(BF16)
    return high, middle, low


def write_toeplitz(shifts_ref, emission_ref, absorption_ref, mix_ref, energy_devs, k_devs):
    count = mix_ref.shape[1] // 4
    points = shifts_ref.shape[1]
    spot = lax.broadcasted_iota(jnp.int32, (2 * count, points), 0)
    shift = shifts_ref[...]
    hit = jnp.where(spot < count, spot, 2 * count - spot) == shift
    onehot = jnp.where(hit, 1.0, 0.0).astype(BF16)
    pieces = in_three(emission_ref[...]) + in_three(absorption_ref[...])
    rows = jnp.concatenate([p.astype(F32) for p in pieces] + [jnp.zeros((2, points), F32)], axis=0)
    sums = lax.dot_general(
        rows.astype(BF16), onehot, (((1,), (1,)), ((), ())), preferred_element_type=F32
    )
    emit = sums[0:1] + sums[1:2] + sums[2:3]
    absorb = sums[3:4] + sums[4:5] + sums[5:6]
    lane = lax.broadcasted_iota(jnp.int32, (1, 2 * count), 1)
    for which, period in enumerate(
        (jnp.where(lane < count, absorb, emit), jnp.where(lane < count, emit, absorb))
    ):
        square = jnp.broadcast_to(period, (count, 2 * count))
        skewed = pltpu.roll(square, 0, 1, stride=1, stride_axis=0)[:, :count]
        high = skewed.astype(BF16).astype(F32)
        for side, piece in enumerate((high, skewed - high)):
            blocks = piece[None]
            blocks = jnp.broadcast_to(
                blocks, (k_devs, count, count)
            ).reshape(k_devs * count, count)
            first = (2 * side + which) * count
            mix_ref[:, first : first + count] = blocks.astype(BF16)


def strided(ref, tiles, first, count, step):
    return jnp.concatenate([ref[t, pl.ds(first, count, stride=step), :] for t in tiles], axis=1)


def layer_kernel(
    has_prev,
    count_ref,
    trans_hbm,
    kweight_hbm,
    shifts_hbm,
    emission_hbm,
    absorption_hbm,
    levels_hbm,
    sigma_hbm,
    broad_hbm,
    occ_hbm,
    src_hbm,
    basis_hbm,
    *rest,
):
    if has_prev:
        prev_hbm, coupling_hbm, send_ref, mix_ref, psi_ref, *rest, prev_ref, coupling_ref = rest
    else:
        send_ref, mix_ref, *rest = rest
    (
        trans_ref,
        kweight_ref,
        shifts_ref,
        emission_ref,
        absorption_ref,
        levels_ref,
        sigma_ref,
        broad_ref,
        occ_ref,
        src_ref,
        basis_ref,
        g_ref,
        y_ref,
        z_ref,
        x_ref,
        sems,
    ) = rest
    kcount, ecount, modes, width = src_ref.shape[2:]
    rows = kcount * ecount * modes
    chunk = chunk_of(width)
    parts = width // chunk
    lanes = y_ref.shape[2]

    pairs = [
        (shifts_hbm, shifts_ref),
        (emission_hbm, emission_ref),
        (absorption_hbm, absorption_ref),
        (trans_hbm, trans_ref),
        (kweight_hbm, kweight_ref),
        (levels_hbm, levels_ref),
        (sigma_hbm, sigma_ref),
        (broad_hbm, broad_ref),
        (occ_hbm, occ_ref),
        (src_hbm, src_ref),
    ]
    for part in range(parts):
        cols = pl.ds(part * chunk, chunk)
        pairs.append((basis_hbm.at[0, cols, :], basis_ref.at[cols, :]))
    if has_prev:
        pairs += [(prev_hbm, prev_ref), (coupling_hbm, coupling_ref)]
    copies = [pltpu.make_async_copy(a, b, sems.at[i]) for i, (a, b) in enumerate(pairs)]
    small, carried, wide = copies[:9], copies[10 + parts :], copies[9 : 10 + parts]
    for copy in small + wide + carried:
        copy.start()
    for copy in small:
        copy.wait()
    first_energy = lax.axis_index("energy") * ecount
    first_k = lax.axis_index("kpt") * kcount
    energy = (first_energy + lax.broadcasted_iota(jnp.int32, (ecount, 1), 0)).astype(F32)
    energy = (energy + 0.5) * (4.0 / (mix_ref.shape[1] // 4)) - 2.0
    mode = lax.broadcasted_iota(jnp.int32, (1, width), 1)
    active = jnp.where(mode < count_ref[0], 1.0, 0.0)
    base = energy - levels_ref[...] - sigma_ref[0]
    imag = ETA + broad_ref[0]
    imag2 = imag * imag
    for k in range(kcount):
        real = base - trans_ref[k]
        scale = active / (real * real + imag2)
        g_ref[0, k] = real * scale
        g_ref[1, k] = -imag * scale
    write_toeplitz(shifts_ref, emission_ref, absorption_ref, mix_ref, *send_ref.shape[1::-1])

    total = kweight_ref[0]
    for k in range(1, kweight_ref.shape[0]):
        total = total + kweight_ref[k]
    total = jnp.full((ecount, 1), total, jnp.int32).astype(F32)
    weights = [kweight_ref[first_k + k].astype(F32) for k in range(kcount)]
    diagonal = lax.broadcasted_iota(jnp.int32, (ecount, ecount), 0) == lax.broadcasted_iota(
        jnp.int32, (ecount, ecount), 1
    )
    filled = []
    for m in range(modes):
        row = jnp.broadcast_to(occ_ref[m : m + 1, :], (ecount, ecount))
        filled.append(jnp.sum(jnp.where(diagonal, row, 0.0), axis=1, keepdims=True))
    less_of = [f / total for f in filled]
    great_of = [(1.0 - f) / total for f in filled]

    def scale_modes(part):
        cols = pl.ds(part * chunk, chunk)
        tiles = range(part * (chunk // lanes), (part + 1) * (chunk // lanes))
        for k in range(kcount):
            g_real = g_ref[0, k, :, cols]
            g_imag = g_ref[1, k, :, cols]
            z_re = []
            z_im = []
            for m in range(modes):
                first = k * ecount * modes + m
                y_re = strided(y_ref, tiles, first, ecount, modes)
                y_im = strided(y_ref, tiles, rows + first, ecount, modes)
                z_re.append(y_re * g_real - y_im * g_imag)
                z_im.append(y_re * g_imag + y_im * g_real)
            group = pl.ds(k * ecount * modes, ecount * modes)
            z_ref[group, cols] = jnp.concatenate(z_re, axis=0).astype(BF16)
            group = pl.ds(rows + k * ecount * modes, ecount * modes)
            z_ref[group, cols] = jnp.concatenate(z_im, axis=0).astype(BF16)

    copies_k = send_ref.shape[0]
    block = width // send_ref.shape[1]

    def densities(part, psi):
        if has_prev:
            psi_ref[:, pl.ds(part * chunk, chunk)] = psi.astype(BF16)
        less = None
        great = None
        for m in range(modes):
            per_mode = None
            for k in range(kcount):
                first = (k * modes + m) * ecount
                re = psi[first : first + ecount]
                im = psi[rows + first : rows + first + ecount]
                term = (re * re + im * im) * weights[k]
                per_mode = term if per_mode is None else per_mode + term
            less = per_mode * less_of[m] if less is None else less + per_mode * less_of[m]
            great = per_mode * great_of[m] if great is None else great + per_mode * great_of[m]
        for t in range(chunk // block):
            both = jnp.concatenate(
                [less[:, t * block : (t + 1) * block], great[:, t * block : (t + 1) * block]], axis=1
            ).astype(BF16)
            for c in range(copies_k):
                send_ref[c, part * (chunk // block) + t] = both

    wide[0].wait()
    x_ref[...] = src_ref[0].reshape(2 * rows, width)
    if has_prev:
        for copy in carried:
            copy.wait()
        brought = jnp.dot(prev_ref[...], coupling_ref[0], preferred_element_type=F32)
        x_ref[...] = (brought + x_ref[...].astype(F32)).astype(BF16)
    stages = min(2, parts)
    for stage in range(stages):
        first_part = stage * parts // stages
        last_part = (stage + 1) * parts // stages
        for part in range(first_part, last_part):
            wide[1 + part].wait()
        depth = pl.ds(first_part * chunk, (last_part - first_part) * chunk)
        for part in range(parts):
            cols = pl.ds(part * chunk, chunk)
            y_val = jnp.dot(x_ref[:, depth], basis_ref[depth, cols], preferred_element_type=F32)
            for t in range(chunk // lanes):
                tile = part * (chunk // lanes) + t
                piece = y_val[:, t * lanes : (t + 1) * lanes]
                y_ref[tile] = piece if stage == 0 else y_ref[tile] + piece
    for part in range(parts):
        scale_modes(part)
    for part in range(parts):
        psi = lax.dot_general(
            z_ref[...],
            basis_ref[pl.ds(part * chunk, chunk), :],
            (((1,), (1,)), ((), ())),
            preferred_element_type=F32,
        )
        densities(part, psi)


def mix_kernel(got_ref, mix_ref, less_ref, great_ref):
    depth = mix_ref.shape[0]
    count = mix_ref.shape[1] // 4
    dens = got_ref[...].astype(F32).reshape(depth, got_ref.shape[3]).astype(BF16)
    out = lax.dot_general(
        dens, mix_ref[...], (((0,), (0,)), ((), ())), preferred_element_type=F32
    )
    out = out[:, : 2 * count] + out[:, 2 * count :]
    block = less_ref.shape[1]
    less_ref[0] = out[:block, :count]
    great_ref[0] = out[block:, count:]


def on_device(
    source,
    basis,
    coupling,
    levels,
    sigma_real,
    broadening,
    transverse,
    counts,
    occupation,
    kweight,
    shifts,
    emission,
    absorption,
):
    kcount, ecount, modes, width = source.shape[2:]
    rows = kcount * ecount * modes
    energy_devs = lax.axis_size("energy")
    k_devs = lax.axis_size("kpt")
    layer_devs = lax.axis_size("layer")
    all_energies = ecount * energy_devs
    block = width // energy_devs
    parts = width // chunk_of(width)
    vmem = pl.BlockSpec(memory_space=VMEM)
    hbm = pl.BlockSpec(memory_space=pltpu.HBM)
    operands = (
        counts,
        transverse,
        kweight,
        shifts[None],
        emission[None],
        absorption[None],
        levels,
        sigma_real,
        broadening,
        occupation.T,
        source,
        basis,
    )
    send_shape = jax.ShapeDtypeStruct((k_devs, energy_devs, ecount, 2 * block), BF16)
    mix_shape = jax.ShapeDtypeStruct((k_devs * all_energies, 4 * all_energies), BF16)
    scratch = (
        [SMEM(a.shape, a.dtype) for a in operands[1:3]]
        + [VMEM(a.shape, a.dtype) for a in operands[3:11]]
        + [
            VMEM((width, width), BF16),
            VMEM((2, kcount, ecount, width), F32),
            VMEM((width // 128, 2 * rows, 128), F32),
            VMEM((2 * rows, width), BF16),
            VMEM((2 * rows, width), BF16),
        ]
    )
    psi_shape = jax.ShapeDtypeStruct((2 * rows, width), BF16)

    def layer(prev):
        has_prev = prev is not None
        more = (prev, coupling) if has_prev else ()
        in_hbm = [pltpu.with_memory_space_constraint(a, pltpu.HBM) for a in operands[1:] + more]
        sems = pltpu.SemaphoreType.DMA((10 + parts + len(more),))
        return pl.pallas_call(
            functools.partial(layer_kernel, has_prev),
            out_shape=(send_shape, mix_shape) + ((psi_shape,) if has_prev else ()),
            in_specs=[pl.BlockSpec(memory_space=SMEM)] + [hbm] * len(in_hbm),
            out_specs=(vmem,) * (3 if has_prev else 2),
            scratch_shapes=scratch + [sems] + [VMEM(a.shape, a.dtype) for a in more],
            compiler_params=pltpu.CompilerParams(vmem_limit_bytes=24 * 1024 * 1024),
        )(operands[0], *in_hbm)

    if layer_devs == 1:
        send, mix = layer(None)
    else:
        layer_pos = lax.axis_index("layer")

        def sweep(step, state):
            carry, kept = state
            kept = lax.cond(step == layer_pos, lambda: tuple(layer(carry)), lambda: kept)
            carry = kept[2].reshape(2, kcount, modes, ecount, width).transpose(0, 1, 3, 2, 4)
            carry = from_behind(carry.reshape(2 * rows, width), "layer", 1)
            return carry, kept

        stored = tuple(jnp.zeros(a.shape, a.dtype) for a in (send_shape, mix_shape, psi_shape))
        send, mix, _ = lax.fori_loop(0, layer_devs, sweep, (stored[2], stored))[1]
    got = lax.all_to_all(
        send.reshape(energy_devs * k_devs, ecount, 2 * block), ("kpt", "energy"), 0, 0, tiled=True
    ).reshape(k_devs, energy_devs, ecount, 2 * block)
    out_shape = jax.ShapeDtypeStruct((1, block, all_energies), F32)
    return pl.pallas_call(
        mix_kernel,
        out_shape=(out_shape, out_shape),
        in_specs=[vmem, vmem],
        out_specs=(vmem, vmem),
        compiler_params=pltpu.CompilerParams(vmem_limit_bytes=8 * 1024 * 1024),
    )(got, mix)


def solution(mesh):
    in_specs = (
        P("layer", None, "kpt", "energy", None, None),
        P("layer", None, None),
        P("layer", None, None),
        P("layer", None),
        P("layer", "energy", None),
        P("layer", "energy", None),
        P("kpt"),
        P("layer"),
        P("energy", None),
        P(),
        P(),
        P(),
        P(),
    )
    out_specs = (P("layer", "energy", None), P("layer", "energy", None))
    return jax.shard_map(
        on_device, mesh=mesh, in_specs=in_specs, out_specs=out_specs, check_vma=False
    )
```

```python
import functools

import jax
import jax.numpy as jnp
from jax import lax
from jax.experimental import pallas as pl
from jax.experimental.pallas import tpu as pltpu
from jax.sharding import PartitionSpec as P

ETA = 1.0
F32 = jnp.float32
BF16 = jnp.bfloat16
VMEM = pltpu.VMEM
SMEM = pltpu.SMEM


def from_behind(shard, axis, by):
    size = lax.axis_size(axis)
    pairs = [(i, i + by) for i in range(size) if 0 <= i + by < size]
    return lax.ppermute(shard, axis, pairs)


def chunk_of(width):
    return 512 if width % 512 == 0 else width


def in_three(value):
    high = value.astype(BF16)
    rest = value - high.astype(F32)
    middle = rest.astype(BF16)
    low = (rest - middle.astype(F32)).astype(BF16)
    return high, middle, low


def write_toeplitz(shifts_ref, emission_ref, absorption_ref, mix_ref, energy_devs, k_devs):
    count = mix_ref.shape[1] // 4
    points = shifts_ref.shape[1]
    spot = lax.broadcasted_iota(jnp.int32, (2 * count, points), 0)
    shift = shifts_ref[...]
    hit = jnp.where(spot < count, spot, 2 * count - spot) == shift
    onehot = jnp.where(hit, 1.0, 0.0).astype(BF16)
    pieces = in_three(emission_ref[...]) + in_three(absorption_ref[...])
    rows = jnp.concatenate([p.astype(F32) for p in pieces] + [jnp.zeros((2, points), F32)], axis=0)
    sums = lax.dot_general(
        rows.astype(BF16), onehot, (((1,), (1,)), ((), ())), preferred_element_type=F32
    )
    emit = sums[0:1] + sums[1:2] + sums[2:3]
    absorb = sums[3:4] + sums[4:5] + sums[5:6]
    lane = lax.broadcasted_iota(jnp.int32, (1, 2 * count), 1)
    for which, period in enumerate(
        (jnp.where(lane < count, absorb, emit), jnp.where(lane < count, emit, absorb))
    ):
        square = jnp.broadcast_to(period, (count, 2 * count))
        skewed = pltpu.roll(square, 0, 1, stride=1, stride_axis=0)[:, :count]
        high = skewed.astype(BF16).astype(F32)
        for side, piece in enumerate((high, skewed - high)):
            blocks = piece[None]
            blocks = jnp.broadcast_to(
                blocks, (k_devs, count, count)
            ).reshape(k_devs * count, count)
            first = (2 * side + which) * count
            mix_ref[:, first : first + count] = blocks.astype(BF16)


def strided(ref, tiles, first, count, step):
    return jnp.concatenate([ref[t, pl.ds(first, count, stride=step), :] for t in tiles], axis=1)


def layer_kernel(
    has_prev,
    count_ref,
    trans_hbm,
    kweight_hbm,
    shifts_hbm,
    emission_hbm,
    absorption_hbm,
    levels_hbm,
    sigma_hbm,
    broad_hbm,
    occ_hbm,
    src_hbm,
    basis_hbm,
    *rest,
):
    if has_prev:
        prev_hbm, coupling_hbm, send_ref, mix_ref, psi_ref, *rest, prev_ref, coupling_ref = rest
    else:
        send_ref, mix_ref, *rest = rest
    (
        trans_ref,
        kweight_ref,
        shifts_ref,
        emission_ref,
        absorption_ref,
        levels_ref,
        sigma_ref,
        broad_ref,
        occ_ref,
        src_ref,
        basis_ref,
        g_ref,
        y_ref,
        z_ref,
        x_ref,
        sems,
    ) = rest
    kcount, ecount, modes, width = src_ref.shape[2:]
    rows = kcount * ecount * modes
    chunk = chunk_of(width)
    parts = width // chunk
    lanes = y_ref.shape[2]

    pairs = [
        (shifts_hbm, shifts_ref),
        (emission_hbm, emission_ref),
        (absorption_hbm, absorption_ref),
        (trans_hbm, trans_ref),
        (kweight_hbm, kweight_ref),
        (levels_hbm, levels_ref),
        (sigma_hbm, sigma_ref),
        (broad_hbm, broad_ref),
        (occ_hbm, occ_ref),
        (src_hbm, src_ref),
    ]
    for part in range(parts):
        cols = pl.ds(part * chunk, chunk)
        pairs.append((basis_hbm.at[0, cols, :], basis_ref.at[cols, :]))
    if has_prev:
        pairs += [(prev_hbm, prev_ref), (coupling_hbm, coupling_ref)]
    copies = [pltpu.make_async_copy(a, b, sems.at[i]) for i, (a, b) in enumerate(pairs)]
    small, carried, wide = copies[:9], copies[10 + parts :], copies[9 : 10 + parts]
    for copy in small + wide + carried:
        copy.start()
    for copy in small:
        copy.wait()
    first_energy = lax.axis_index("energy") * ecount
    first_k = lax.axis_index("kpt") * kcount
    energy = (first_energy + lax.broadcasted_iota(jnp.int32, (ecount, 1), 0)).astype(F32)
    energy = (energy + 0.5) * (4.0 / (mix_ref.shape[1] // 4)) - 2.0
    mode = lax.broadcasted_iota(jnp.int32, (1, width), 1)
    active = jnp.where(mode < count_ref[0], 1.0, 0.0)
    base = energy - levels_ref[...] - sigma_ref[0]
    imag = ETA + broad_ref[0]
    imag2 = imag * imag
    for k in range(kcount):
        real = base - trans_ref[k]
        scale = active / (real * real + imag2)
        g_ref[0, k] = real * scale
        g_ref[1, k] = -imag * scale
    write_toeplitz(shifts_ref, emission_ref, absorption_ref, mix_ref, *send_ref.shape[1::-1])

    total = kweight_ref[0]
    for k in range(1, kweight_ref.shape[0]):
        total = total + kweight_ref[k]
    total = jnp.full((ecount, 1), total, jnp.int32).astype(F32)
    weights = [kweight_ref[first_k + k].astype(F32) for k in range(kcount)]
    diagonal = lax.broadcasted_iota(jnp.int32, (ecount, ecount), 0) == lax.broadcasted_iota(
        jnp.int32, (ecount, ecount), 1
    )
    filled = []
    for m in range(modes):
        row = jnp.broadcast_to(occ_ref[m : m + 1, :], (ecount, ecount))
        filled.append(jnp.sum(jnp.where(diagonal, row, 0.0), axis=1, keepdims=True))
    less_of = [f / total for f in filled]
    great_of = [(1.0 - f) / total for f in filled]

    def scale_modes(part):
        cols = pl.ds(part * chunk, chunk)
        tiles = range(part * (chunk // lanes), (part + 1) * (chunk // lanes))
        for k in range(kcount):
            g_real = g_ref[0, k, :, cols]
            g_imag = g_ref[1, k, :, cols]
            z_re = []
            z_im = []
            for m in range(modes):
                first = k * ecount * modes + m
                y_re = strided(y_ref, tiles, first, ecount, modes)
                y_im = strided(y_ref, tiles, rows + first, ecount, modes)
                z_re.append(y_re * g_real - y_im * g_imag)
                z_im.append(y_re * g_imag + y_im * g_real)
            group = pl.ds(k * ecount * modes, ecount * modes)
            z_ref[group, cols] = jnp.concatenate(z_re, axis=0).astype(BF16)
            group = pl.ds(rows + k * ecount * modes, ecount * modes)
            z_ref[group, cols] = jnp.concatenate(z_im, axis=0).astype(BF16)

    copies_k = send_ref.shape[0]
    block = width // send_ref.shape[1]

    def densities(part, psi):
        if has_prev:
            psi_ref[:, pl.ds(part * chunk, chunk)] = psi.astype(BF16)
        less = None
        great = None
        for m in range(modes):
            per_mode = None
            for k in range(kcount):
                first = (k * modes + m) * ecount
                re = psi[first : first + ecount]
                im = psi[rows + first : rows + first + ecount]
                term = (re * re + im * im) * weights[k]
                per_mode = term if per_mode is None else per_mode + term
            less = per_mode * less_of[m] if less is None else less + per_mode * less_of[m]
            great = per_mode * great_of[m] if great is None else great + per_mode * great_of[m]
        for t in range(chunk // block):
            both = jnp.concatenate(
                [less[:, t * block : (t + 1) * block], great[:, t * block : (t + 1) * block]], axis=1
            ).astype(BF16)
            for c in range(copies_k):
                send_ref[c, part * (chunk // block) + t] = both

    wide[0].wait()
    x_ref[...] = src_ref[0].reshape(2 * rows, width)
    if has_prev:
        for copy in carried:
            copy.wait()
        brought = jnp.dot(prev_ref[...], coupling_ref[0], preferred_element_type=F32)
        x_ref[...] = (brought + x_ref[...].astype(F32)).astype(BF16)
    stages = min(2, parts)
    for stage in range(stages):
        first_part = stage * parts // stages
        last_part = (stage + 1) * parts // stages
        for part in range(first_part, last_part):
            wide[1 + part].wait()
        depth = pl.ds(first_part * chunk, (last_part - first_part) * chunk)
        for part in range(parts):
            cols = pl.ds(part * chunk, chunk)
            y_val = jnp.dot(x_ref[:, depth], basis_ref[depth, cols], preferred_element_type=F32)
            for t in range(chunk // lanes):
                tile = part * (chunk // lanes) + t
                piece = y_val[:, t * lanes : (t + 1) * lanes]
                y_ref[tile] = piece if stage == 0 else y_ref[tile] + piece
    for part in range(parts):
        scale_modes(part)
    for part in range(parts):
        psi = lax.dot_general(
            z_ref[...],
            basis_ref[pl.ds(part * chunk, chunk), :],
            (((1,), (1,)), ((), ())),
            preferred_element_type=F32,
        )
        densities(part, psi)


def mix_kernel(got_ref, mix_ref, less_ref, great_ref):
    depth = mix_ref.shape[0]
    count = mix_ref.shape[1] // 4
    dens = got_ref[...].astype(F32).reshape(depth, got_ref.shape[3]).astype(BF16)
    out = lax.dot_general(
        dens, mix_ref[...], (((0,), (0,)), ((), ())), preferred_element_type=F32
    )
    out = out[:, : 2 * count] + out[:, 2 * count :]
    block = less_ref.shape[1]
    less_ref[0] = out[:block, :count]
    great_ref[0] = out[block:, count:]


def on_device(
    source,
    basis,
    coupling,
    levels,
    sigma_real,
    broadening,
    transverse,
    counts,
    occupation,
    kweight,
    shifts,
    emission,
    absorption,
):
    kcount, ecount, modes, width = source.shape[2:]
    rows = kcount * ecount * modes
    energy_devs = lax.axis_size("energy")
    k_devs = lax.axis_size("kpt")
    layer_devs = lax.axis_size("layer")
    all_energies = ecount * energy_devs
    block = width // energy_devs
    parts = width // chunk_of(width)
    vmem = pl.BlockSpec(memory_space=VMEM)
    hbm = pl.BlockSpec(memory_space=pltpu.HBM)
    operands = (
        counts,
        transverse,
        kweight,
        shifts[None],
        emission[None],
        absorption[None],
        levels,
        sigma_real,
        broadening,
        occupation.T,
        source,
        basis,
    )
    send_shape = jax.ShapeDtypeStruct((k_devs, energy_devs, ecount, 2 * block), BF16)
    mix_shape = jax.ShapeDtypeStruct((k_devs * all_energies, 4 * all_energies), BF16)
    scratch = (
        [SMEM(a.shape, a.dtype) for a in operands[1:3]]
        + [VMEM(a.shape, a.dtype) for a in operands[3:11]]
        + [
            VMEM((width, width), BF16),
            VMEM((2, kcount, ecount, width), F32),
            VMEM((width // 128, 2 * rows, 128), F32),
            VMEM((2 * rows, width), BF16),
            VMEM((2 * rows, width), BF16),
        ]
    )
    psi_shape = jax.ShapeDtypeStruct((2 * rows, width), BF16)

    def layer(prev):
        has_prev = prev is not None
        more = (prev, coupling) if has_prev else ()
        in_hbm = [pltpu.with_memory_space_constraint(a, pltpu.HBM) for a in operands[1:] + more]
        sems = pltpu.SemaphoreType.DMA((10 + parts + len(more),))
        return pl.pallas_call(
            functools.partial(layer_kernel, has_prev),
            out_shape=(send_shape, mix_shape) + ((psi_shape,) if has_prev else ()),
            in_specs=[pl.BlockSpec(memory_space=SMEM)] + [hbm] * len(in_hbm),
            out_specs=(vmem,) * (3 if has_prev else 2),
            scratch_shapes=scratch + [sems] + [VMEM(a.shape, a.dtype) for a in more],
            compiler_params=pltpu.CompilerParams(vmem_limit_bytes=24 * 1024 * 1024),
        )(operands[0], *in_hbm)

    if layer_devs == 1:
        send, mix = layer(None)
    else:
        layer_pos = lax.axis_index("layer")

        def sweep(step, state):
            carry, kept = state
            kept = lax.cond(step == layer_pos, lambda: tuple(layer(carry)), lambda: kept)
            carry = kept[2].reshape(2, kcount, modes, ecount, width).transpose(0, 1, 3, 2, 4)
            carry = from_behind(carry.reshape(2 * rows, width), "layer", 1)
            return carry, kept

        stored = tuple(jnp.zeros(a.shape, a.dtype) for a in (send_shape, mix_shape, psi_shape))
        send, mix, _ = lax.fori_loop(0, layer_devs, sweep, (stored[2], stored))[1]
    got = lax.all_to_all(
        send.reshape(energy_devs * k_devs, ecount, 2 * block), ("kpt", "energy"), 0, 0, tiled=True
    ).reshape(k_devs, energy_devs, ecount, 2 * block)
    out_shape = jax.ShapeDtypeStruct((1, block, all_energies), F32)
    return pl.pallas_call(
        mix_kernel,
        out_shape=(out_shape, out_shape),
        in_specs=[vmem, vmem],
        out_specs=(vmem, vmem),
        compiler_params=pltpu.CompilerParams(vmem_limit_bytes=8 * 1024 * 1024),
    )(got, mix)


def solution(mesh):
    in_specs = (
        P("layer", None, "kpt", "energy", None, None),
        P("layer", None, None),
        P("layer", None, None),
        P("layer", None),
        P("layer", "energy", None),
        P("layer", "energy", None),
        P("kpt"),
        P("layer"),
        P("energy", None),
        P(),
        P(),
        P(),
        P(),
    )
    out_specs = (P("layer", "energy", None), P("layer", "energy", None))
    return jax.shard_map(
        on_device, mesh=mesh, in_specs=in_specs, out_specs=out_specs, check_vma=False
    )
```
